32 devices in a mesh: row: 8 (over z, x), col: 4 (over y, core).
Axes of the slice: x: 2, y: 2, z: 4, core: 2. Of those that a mesh axis runs over, the one named last changes fastest.
Arguments:
- front_tiles: bfloat16 [4, 2048, 2, 1024], P(None, 'row', None, 'col'), may hold values from -6 to 6
- fill_pattern: int32 [4, 8, 2, 4], P(None, 'row', None, 'col'), may hold values from 0 to 1, as said below
- w_inverse: bfloat16 [2, 256, 256], replicated, may hold values from -0.015625 to 0.015625
- samples: bfloat16 [4, 2048, 512], P(None, 'row'), may hold values from -6 to 6
Outputs:
- factor_slab: bfloat16 [4, 2048, 2, 1024], P(None, 'row', None, 'col')
- solved_rows: bfloat16 [4, 2048, 512], P(None, 'row')
The draws below stay inside these ranges and needn't reach their ends.
Inputs may be any that keep to these rules, and one draw needn't show every extreme that they name: With i and j as in the reference program, fill_pattern[a, r, b, c] is 1 exactly when first(i) <= j <= i, for a first column first(i) of tile row i with first(0) = first(1) = 0.
All inputs are finite; a program needn't handle non-finite values.
Results may differ from the reference program's by a relative error of at most 0.0062.
Values may be sent and summed in bfloat16 or wider, within the bound.
A program may use at most 64 MiB of HBM per device.

```python
import jax
import jax.numpy as jnp

B = 256
S = 512
TR = 4
TC = 2
NT = 32
NCOL = 8
N_ROW = 8
N_COL = 4


def draw_fill_pattern(key, part):
    rows_per = NT // TR
    cols_per = NCOL // TC
    tile_rows = jnp.arange(TR)[:, None] * rows_per + jnp.arange(rows_per)[None, :]
    tile_cols = jnp.arange(TC)[:, None] * cols_per + jnp.arange(cols_per)[None, :]
    key_coin, key_first = jax.random.split(jax.random.fold_in(key, 7))
    coin_flip = jax.random.randint(key_coin, (TR, rows_per), 0, 2)
    start_col = jax.random.randint(key_first, (TR, rows_per), 0, tile_rows + 1)
    first_col = jnp.where((coin_flip == 0) | (tile_rows < 2), 0, start_col)
    row_grid = tile_rows[:, :, None, None]
    col_grid = tile_cols[None, None, :, :]
    inside = (col_grid >= first_col[:, :, None, None]) & (col_grid <= row_grid)
    return inside.astype(jnp.int32)


def draw_w_inverse(key, part):
    key_rows, key_cols = jax.random.split(jax.random.fold_in(key, 11))
    index_line = jnp.arange(B)
    parity = jnp.zeros((B, B), jnp.int32)
    bit_count = B.bit_length() - 1
    for bit_pos in range(bit_count):
        stride = 2 ** bit_pos
        parity = parity + index_line[:, None] // stride % 2 * (index_line[None, :] // stride % 2)
    signed_table = (1 - 2 * (parity % 2)).astype(jnp.float32)
    row_signs = (2 * jax.random.randint(key_rows, (2, B, 1), 0, 2) - 1).astype(jnp.float32)
    col_signs = (2 * jax.random.randint(key_cols, (2, 1, B), 0, 2) - 1).astype(jnp.float32)
    magnitude = 0.25 / jnp.sqrt(jnp.float32(B))
    return (signed_table[None, :, :] * row_signs * col_signs * magnitude).astype(jnp.bfloat16)


def shard_levels(own_key, dims, cuts, least, high):
    def one(axis_at, parts):
        steps = jax.random.uniform(jax.random.fold_in(jax.random.fold_in(own_key, 6), axis_at), (parts,), jnp.float32, least / len(cuts), high / len(cuts))
        return jnp.repeat(jnp.exp(steps), dims[axis_at] // parts).reshape((-1,) + (1,) * (len(dims) - axis_at - 1))

    level = one(*cuts[0])
    for cut in cuts[1:]:
        level = level * one(*cut)
    return level


def centred(own_key, shape, scale, bound, cuts=(), kind=jnp.bfloat16):
    loudness = shard_levels(own_key, shape, cuts, -0.22, 0.18) if cuts else 1.0
    entries = jax.random.normal(own_key, shape, jnp.float32) * scale * loudness
    return jnp.minimum(jnp.maximum(entries, -bound), bound).astype(kind)


def setup_inputs(seed: int = 0) -> dict:
    arg_keys = jax.random.split(jax.random.key(seed), 5)
    return {
        "front_tiles": centred(arg_keys[0], (TR, B * N_ROW, TC, B * N_COL), 1.0, 6.0, ((1, 8), (3, 4))),
        "fill_pattern": draw_fill_pattern(jax.random.fold_in(arg_keys[4], 71), 0),
        "w_inverse": draw_w_inverse(jax.random.fold_in(arg_keys[4], 71), 0),
        "samples": centred(arg_keys[3], (TR, B * N_ROW, S), 1.0, 6.0, ((1, 8),)),
    }


def reference(front_tiles, fill_pattern, w_inverse, samples):
    tiled_view = front_tiles.reshape(TR, N_ROW, B, TC, N_COL, B)
    pattern = fill_pattern.reshape(TR, N_ROW, 1, TC, N_COL, 1).astype(front_tiles.dtype)
    masked = tiled_view * pattern
    tile_row = (jnp.arange(TR)[:, None] * N_ROW + jnp.arange(N_ROW)[None, :]).reshape(NT)
    first_col = masked[:, :, :, 0, 0, :].reshape(NT, B, B)
    second_col = masked[:, :, :, 0, 1, :].reshape(NT, B, B)
    inverse_first = w_inverse[0].astype(jnp.float32)
    inverse_second = w_inverse[1].astype(jnp.float32)
    first_panel = jnp.einsum("ikm,mn->ikn", first_col.astype(jnp.float32), inverse_first)
    first_panel = jnp.where(tile_row[:, None, None] >= 1, first_panel, 0.0).astype(jnp.bfloat16)
    updated_second = second_col.astype(jnp.float32) - jnp.einsum(
        "ikm,nm->ikn", first_panel.astype(jnp.float32), first_panel[1].astype(jnp.float32))
    updated_second = updated_second.astype(jnp.bfloat16)
    second_panel = jnp.einsum("ikm,mn->ikn", updated_second.astype(jnp.float32), inverse_second)
    second_panel = jnp.where(tile_row[:, None, None] >= 2, second_panel, 0.0).astype(jnp.bfloat16)
    both_rows = jnp.concatenate([first_panel, second_panel], axis=2)
    both_cols = both_rows[:NCOL].reshape(TC, N_COL, B, 2 * B).astype(jnp.float32)
    rows_view = both_rows.reshape(TR, N_ROW, B, 2 * B)
    blocks = []
    for group_idx in range(TR):
        rows_here = rows_view[group_idx].astype(jnp.float32)
        product = jnp.einsum("rkm,bcnm->rkbcn", rows_here, both_cols)
        block_out = (masked[group_idx].astype(jnp.float32) - product) * pattern[group_idx].astype(jnp.float32)
        blocks.append(block_out.astype(jnp.bfloat16))
    trailing = jnp.stack(blocks)
    lead_first = jnp.where(tile_row[:, None, None] >= 1, first_panel, first_col)
    lead_second = jnp.where(tile_row[:, None, None] >= 2, second_panel, updated_second)
    trailing = trailing.at[:, :, :, 0, 0, :].set(lead_first.reshape(TR, N_ROW, B, B))
    trailing = trailing.at[:, :, :, 0, 1, :].set(lead_second.reshape(TR, N_ROW, B, B))
    factor_slab = trailing.reshape(TR, N_ROW * B, TC, N_COL * B)

    rhs_tiles = samples.reshape(NT, B, S)
    first_solve = jnp.dot(w_inverse[0].T, rhs_tiles[0], preferred_element_type=jnp.float32).astype(jnp.bfloat16)
    reduced = (rhs_tiles[1].astype(jnp.float32)
               - jnp.dot(first_panel[1], first_solve, preferred_element_type=jnp.float32)).astype(jnp.bfloat16)
    second_solve = jnp.dot(w_inverse[1].T, reduced, preferred_element_type=jnp.float32).astype(jnp.bfloat16)
    stacked = jnp.concatenate([first_solve, second_solve], axis=0).astype(jnp.float32)
    remaining = rhs_tiles.astype(jnp.float32) - jnp.einsum("ikm,ms->iks", both_rows.astype(jnp.float32), stacked)
    remaining = remaining.astype(jnp.bfloat16)
    remaining = remaining.at[0].set(first_solve)
    remaining = remaining.at[1].set(second_solve)
    solved_rows = remaining.reshape(TR, N_ROW * B, S)
    return (factor_slab, solved_rows)
```

```python
import functools

import jax
import jax.numpy as jnp
from jax import lax
from jax.experimental import pallas as pl
from jax.experimental.pallas import tpu as pltpu
from jax.sharding import PartitionSpec as P

MESH = pl.DeviceIdType.MESH
F32 = jnp.float32
BF16 = jnp.bfloat16


def dot_nn(a, b):
    return jnp.dot(a, b, preferred_element_type=F32)


def dot_nt(a, b):
    return lax.dot_general(a, b, (((1,), (1,)), ((), ())), preferred_element_type=F32)


def kernel(R, C, fm, w, smp, out, sol, rowf, colf, f10, sbuf, cols, rows, ys, l01,
           y_s, y_r, b_s, b_r, cu_s, cd_s, cx_s, c_r, fs_s, su_s, sx_s, sb_s, s_r, sb_r):
    A, TC, B, _ = fm.shape
    Q = R // 2
    Y = C // 2
    half = B // 2
    r, c = lax.axis_index("row"), lax.axis_index("col")
    q, x, yy, k = r // 2, r % 2, c // 2, c % 2
    sib = c + 1 - 2 * k
    mate = r + 1 - 2 * x
    pending = []

    def desc(src, dst, ss, rs, row, col):
        return pltpu.make_async_remote_copy(
            src_ref=src, dst_ref=dst, send_sem=ss, recv_sem=rs,
            device_id={"row": row, "col": col}, device_id_type=MESH)

    def send(cond, src, dst, ss, rs, row, col):
        copy = desc(src, dst, ss, rs, row, col)
        pending.append((cond, copy))

        @pl.when(cond)
        def _():
            copy.start()

    def arrive(cond, dst, rs):
        @pl.when(cond)
        def _():
            desc(dst, dst, fs_s.at[0], rs, r, sib).wait_recv()

    barrier = pltpu.get_barrier_semaphore()
    has_up, has_dn = q + 1 < Q, q > 0
    has_yu, has_yd = yy + 1 < Y, yy > 0
    true = r >= 0
    for cond, row, col in ((true, r, sib), (true, mate, c), (has_up, r + 2, c), (has_dn, r - 2, c),
                           (has_yu, r, c + 2), (has_yd, r, c - 2)):
        @pl.when(cond)
        def _():
            pl.semaphore_signal(barrier, inc=1, device_id={"row": row, "col": col}, device_id_type=MESH)
    ends = (q + 1 < Q).astype(jnp.int32) + (q > 0).astype(jnp.int32)
    ends = ends + (yy + 1 < Y).astype(jnp.int32) + (yy > 0).astype(jnp.int32)
    pl.semaphore_wait(barrier, 2 + ends)

    lead = yy == 0
    later = yy > 0

    for a in range(A):
        send(lead, fm.at[a, 0], rowf.at[k, a], b_s.at[a], b_r.at[a], r, sib)
        send(lead & has_yu, fm.at[a, 0], rowf.at[k, a], y_s.at[a], y_r.at[a], r, c + 2)

    mine = pl.ds(pl.multiple_of(k * half, half), half)
    other = pl.ds(pl.multiple_of((1 - k) * half, half), half)
    s_root = q == 0
    piece = smp.at[0, mine]
    send(s_root & has_up, piece, sbuf.at[x, mine], su_s.at[0], s_r.at[x], r + 2, c)
    send(s_root, piece, sbuf.at[x, mine], sx_s.at[0], s_r.at[x], mate, c)

    @pl.when(s_root)
    def _():
        sbuf[x] = smp[0]

    @pl.when(lead)
    def _():
        for a in range(A):
            rowf[k, a] = fm[a, 0]

    def row_tile(a):
        arrive(later, rowf.at[k, a], y_r.at[a])
        send(later, rowf.at[k, a], rowf.at[k, a], b_s.at[a], b_r.at[a], r, sib)
        send(later & has_yu, rowf.at[k, a], rowf.at[k, a], y_s.at[a], y_r.at[a], r, c + 2)

    def row_other(a):
        arrive(true, rowf.at[1 - k, a], b_r.at[a])

    line = x == k

    def root_of(b):
        return (b * C + c) % R

    def col_sends(cond, b, kk, qr):
        src = colf.at[b, kk]
        at = b * 2 + kk
        send(cond & line & has_up & (q >= qr), src, src, cu_s.at[at], c_r.at[at], r + 2, c)
        send(cond & line & has_dn & (q <= qr), src, src, cd_s.at[at], c_r.at[at], r - 2, c)
        send(cond & line, src, src, cx_s.at[at], c_r.at[at], mate, c)

    def col_item(b, kk):
        root = root_of(b)
        at = b * 2 + kk
        away = r != root
        arrive(away, colf.at[b, kk], c_r.at[at])
        col_sends(away, b, kk, root // 2)

    def col_roots(kk):
        for b in range(TC):
            root = root_of(b)

            @pl.when(r == root)
            def _():
                colf[b, kk] = rowf[kk, 0]
            col_sends(r == root, b, kk, root // 2)

    row_tile(0)
    col_roots(k)
    row_other(0)
    col_roots(1 - k)

    f_at = 2 * TC
    f_root = (r == 1) & (k == 1)
    f_line = (x == 1) & (k == 1)

    @pl.when(f_root)
    def _():
        f10[...] = rowf[0, 0]
    send(f_root & has_up, f10, f10, cu_s.at[f_at], c_r.at[f_at], r + 2, c)
    send(f_root, f10, f10, cx_s.at[f_at], c_r.at[f_at], mate, c)
    send(f_root, f10, f10, fs_s.at[0], c_r.at[f_at], r, sib)

    def sample_item(h, on_line):
        got = sbuf.at[h, mine]
        cond = (q > 0) if on_line else true
        arrive(cond, got, s_r.at[h])
        if on_line:
            send(cond & has_up, got, got, su_s.at[1], s_r.at[h], r + 2, c)
            send(cond, got, got, sx_s.at[1], s_r.at[h], mate, c)
        send(cond, got, got, sb_s.at[h], sb_r.at[h], r, sib)

    sample_item(x, True)

    if TC > 1:
        d0, d1 = jnp.abs(q - root_of(0) // 2), jnp.abs(q - root_of(1) // 2)
        first = jnp.where(d0 <= d1, 0, 1)
    else:
        first = 0
    col_item(first, k)
    col_item(first, 1 - k)
    if A > 1:
        row_tile(1)

    f_away = (k == 1) & (r != 1)
    arrive((k == 0) | f_away, f10, c_r.at[f_at])
    send(f_away & f_line & has_up, f10, f10, cu_s.at[f_at], c_r.at[f_at], r + 2, c)
    send(f_away & f_line, f10, f10, cx_s.at[f_at], c_r.at[f_at], mate, c)
    send(f_away, f10, f10, fs_s.at[0], c_r.at[f_at], r, sib)

    sample_item(1 - x, False)
    for t in range(1, TC):
        b = (first + t) % TC
        col_item(b, k)
        col_item(b, 1 - k)
    for a in range(2, A):
        row_tile(a)

    w0, w1 = w[0], w[1]
    l01[...] = dot_nn(f10[...], w0).astype(BF16)
    for b in range(TC):
        j = b * C + c
        f0 = (j >= 1).astype(F32)
        f1 = (j >= 2).astype(F32)
        c0 = (dot_nn(colf[b, 0], w0) * f0).astype(BF16)
        u = (colf[b, 1].astype(F32) - dot_nt(c0, l01[...])).astype(BF16)
        c1 = (dot_nn(u, w1) * f1).astype(BF16)
        cols[b, :, 0:B] = c0
        cols[b, :, B:2 * B] = c1

    arrive((q > 0) | (x != 0), sbuf.at[0, other], sb_r.at[0])
    arrive((q > 0) | (x != 1), sbuf.at[1, other], sb_r.at[1])
    w0t = w0.astype(F32).T.astype(BF16)
    w1t = w1.astype(F32).T.astype(BF16)
    y0 = dot_nn(w0t, sbuf[0]).astype(BF16)
    ys[0:B, :] = y0
    r1 = (sbuf[1].astype(F32) - dot_nn(l01[...], y0)).astype(BF16)
    ys[B:2 * B, :] = dot_nn(w1t, r1).astype(BF16)

    for a in range(1, A):
        row_other(a)

    def tile_row(a, carry):
        i = a * R + r
        f0 = (i >= 1).astype(F32)
        f1 = (i >= 2).astype(F32)
        p0 = (dot_nn(rowf[0, a], w[0]) * f0).astype(BF16)
        u = (rowf[1, a].astype(F32) - dot_nt(p0, l01[...])).astype(BF16)
        p1 = (dot_nn(u, w[1]) * f1).astype(BF16)
        rows[:, 0:B] = p0
        rows[:, B:2 * B] = p1
        for b in range(TC):
            out[a, b] = (fm[a, b].astype(F32) - dot_nt(rows[...], cols[b])).astype(BF16)
        sol[a] = (smp[a].astype(F32) - dot_nn(rows[...], ys[...])).astype(BF16)

        @pl.when((c == 0) & (i >= 1))
        def _():
            out[a, 0] = p0

        @pl.when((c == 0) & (i < 1))
        def _():
            out[a, 0] = rowf[0, a]

        @pl.when((c == 1) & (i >= 2))
        def _():
            out[a, 0] = p1

        @pl.when((c == 1) & (i < 2))
        def _():
            out[a, 0] = u

        @pl.when(i == 0)
        def _():
            sol[a] = ys[0:B, :]

        @pl.when(i == 1)
        def _():
            sol[a] = ys[B:2 * B, :]
        return carry

    lax.fori_loop(0, A, tile_row, 0)

    for cond, copy in pending:
        @pl.when(cond)
        def _():
            copy.wait_send()


def body(R, C, front_tiles, fill_pattern, w_inverse, samples):
    A, B, TC, _ = front_tiles.shape
    S = samples.shape[2]
    assert R % 2 == 0 and C % 2 == 0 and TC * C <= R and TC <= 2
    on = fill_pattern.reshape(A, 1, TC, 1) != 0
    zero = jnp.zeros((), BF16)
    fm = jnp.where(on, front_tiles, zero).transpose(0, 2, 1, 3)
    dma = pltpu.SemaphoreType.DMA
    vmem = pl.BlockSpec(memory_space=pltpu.VMEM)
    out, sol = pl.pallas_call(
        functools.partial(kernel, R, C),
        out_shape=(jax.ShapeDtypeStruct((A, TC, B, B), BF16), jax.ShapeDtypeStruct((A, B, S), BF16)),
        in_specs=[vmem] * 3,
        out_specs=(vmem, vmem),
        scratch_shapes=[
            pltpu.VMEM((2, A, B, B), BF16),
            pltpu.VMEM((TC, 2, B, B), BF16),
            pltpu.VMEM((B, B), BF16),
            pltpu.VMEM((2, B, S), BF16),
            pltpu.VMEM((TC, B, 2 * B), BF16),
            pltpu.VMEM((B, 2 * B), BF16),
            pltpu.VMEM((2 * B, S), BF16),
            pltpu.VMEM((B, B), BF16),
            dma((A,)), dma((A,)), dma((A,)), dma((A,)),
            dma((2 * TC + 1,)), dma((2 * TC + 1,)), dma((2 * TC + 1,)), dma((2 * TC + 1,)),
            dma((1,)), dma((2,)), dma((2,)), dma((2,)), dma((2,)), dma((2,)),
        ],
        compiler_params=pltpu.CompilerParams(
            collective_id=0, has_side_effects=True, vmem_limit_bytes=32 * 1024 * 1024),
        name="panels",
    )(fm, w_inverse, samples)
    factor = jnp.where(on, out.transpose(0, 2, 1, 3), zero)
    return factor, sol


def solution(mesh):
    R, C = mesh.shape["row"], mesh.shape["col"]
    in_specs = (P(None, "row", None, "col"), P(None, "row", None, "col"), P(), P(None, "row", None))
    out_specs = (P(None, "row", None, "col"), P(None, "row", None))
    return jax.shard_map(functools.partial(body, R, C), mesh=mesh, in_specs=in_specs,
                         out_specs=out_specs, check_vma=False)
```

```python
import functools

import jax
import jax.numpy as jnp
from jax import lax
from jax.experimental import pallas as pl
from jax.experimental.pallas import tpu as pltpu
from jax.sharding import PartitionSpec as P

MESH = pl.DeviceIdType.MESH
F32 = jnp.float32
BF16 = jnp.bfloat16


def dot_nn(a, b):
    return jnp.dot(a, b, preferred_element_type=F32)


def dot_nt(a, b):
    return lax.dot_general(a, b, (((1,), (1,)), ((), ())), preferred_element_type=F32)


def kernel(R, C, fm, w, smp, out, sol, rowf, colf, f10, sbuf, cols, rows, ys, l01,
           y_s, y_r, b_s, b_r, cz_s, cx_s, c_r, fz_s, fx_s, f_r, sz_s, s_s, s_r, sb_r):
    A, TC, B, _ = fm.shape
    Q = R // 2
    Y = C // 2
    half = B // 2
    r, c = lax.axis_index("row"), lax.axis_index("col")
    q, x, yy, k = r // 2, r % 2, c // 2, c % 2
    sib = c + 1 - 2 * k
    mate = r + 1 - 2 * x
    line_col = 2 * yy + x
    pending = []

    def desc(src, dst, ss, rs, row, col):
        return pltpu.make_async_remote_copy(
            src_ref=src, dst_ref=dst, send_sem=ss, recv_sem=rs,
            device_id={"row": row, "col": col}, device_id_type=MESH)

    def send(cond, src, dst, ss, rs, row, col):
        copy = desc(src, dst, ss, rs, row, col)
        pending.append((cond, copy))

        @pl.when(cond)
        def _():
            copy.start()

    def arrive(cond, dst, rs):
        @pl.when(cond)
        def _():
            desc(dst, dst, fx_s.at[0], rs, r, sib).wait_recv()

    step = [jnp.where(2 * q < Q, Q - d, d) for d in range(1, Q)]
    away_rows = [2 * lax.rem(q + d, Q) + x for d in step]

    barrier = pltpu.get_barrier_semaphore()
    has_yu, has_yd = yy + 1 < Y, yy > 0
    true = r >= 0
    peers = [(true, r, sib), (true, mate, c), (true, mate, sib), (has_yu, r, c + 2), (has_yd, r, c - 2)]
    for row in away_rows:
        peers += [(true, row, c), (true, row, sib)]
    for cond, row, col in peers:
        @pl.when(cond)
        def _():
            pl.semaphore_signal(barrier, inc=1, device_id={"row": row, "col": col}, device_id_type=MESH)
    ends = (yy + 1 < Y).astype(jnp.int32) + (yy > 0).astype(jnp.int32)
    pl.semaphore_wait(barrier, 3 + 2 * (Q - 1) + ends)

    lead = yy == 0
    later = yy > 0

    for a in range(A):
        send(lead & has_yu, fm.at[a, 0], rowf.at[k, a], y_s.at[a], y_r.at[a], r, c + 2)

    @pl.when(lead)
    def _():
        rowf[k, 0] = fm[0, 0]

    root_b = r // C
    root = (r < TC * C) & ((r % C) // 2 == yy)
    put_b = jnp.where(root, root_b, 0)
    put = colf.at[put_b, k]
    put_sem = c_r.at[put_b * 2 + k]
    f_root = later & (r == 1) & (k == 0)

    def root_sends(cond):
        for n, row in enumerate(away_rows):
            send(cond & root, rowf.at[k, 0], put, cz_s.at[n], put_sem, row, line_col)
        send(cond & root, rowf.at[k, 0], put, cz_s.at[Q - 1], put_sem, mate, line_col)

    def row_tile(a):
        arrive(later, rowf.at[k, a], y_r.at[a])
        send(later, rowf.at[k, a], rowf.at[k, a], b_s.at[a], b_r.at[a], r, sib)
        send(later & has_yu, rowf.at[k, a], rowf.at[k, a], y_s.at[a], y_r.at[a], r, c + 2)

    def row_other(a):
        arrive(true, rowf.at[1 - k, a], b_r.at[a])

    root_sends(lead)
    for a in range(A):
        send(lead, fm.at[a, 0], rowf.at[k, a], b_s.at[a], b_r.at[a], r, sib)

    mine = pl.ds(pl.multiple_of(k * half, half), half)
    other = pl.ds(pl.multiple_of((1 - k) * half, half), half)
    top = yy == Y - 1
    s_root = q == 0
    piece = smp.at[0, mine]
    for n, row in enumerate(away_rows):
        send(s_root & top, piece, sbuf.at[x, mine], sz_s.at[n], s_r.at[x], row, c)
    send(s_root, piece, sbuf.at[x, mine], s_s.at[0], s_r.at[x], mate, c)

    @pl.when(s_root)
    def _():
        sbuf[x] = smp[0]

    @pl.when(lead)
    def _():
        for a in range(1, A):
            rowf[k, a] = fm[a, 0]

    row_tile(0)
    root_sends(later)

    for n, row in enumerate(away_rows):
        send(f_root, rowf.at[0, 0], f10, fz_s.at[n], f_r.at[0], row, c)
    send(f_root, rowf.at[0, 0], f10, fx_s.at[0], f_r.at[0], mate, c)
    send(f_root, rowf.at[0, 0], f10, fx_s.at[1], f_r.at[0], r, sib)

    @pl.when(f_root)
    def _():
        f10[...] = rowf[0, 0]

    def sample_own(cond):
        got = sbuf.at[x, mine]
        cond = cond & (q > 0)
        arrive(cond, got, s_r.at[x])
        send(cond, got, got, s_s.at[1], s_r.at[x], mate, c)
        send(cond & has_yd, got, got, s_s.at[2], s_r.at[x], r, c - 2)
        send(cond, got, got, s_s.at[3], sb_r.at[x], r, sib)

    for a in range(1, min(A, 2)):
        row_tile(a)
    sample_own(later)
    for a in range(2, min(A, 3)):
        row_tile(a)

    f_got = later & (k == 0) & (r != 1)
    arrive(f_got, f10, f_r.at[0])
    send(f_got & (x == 1), f10, f10, fx_s.at[2], f_r.at[0], mate, c)
    send(f_got, f10, f10, fx_s.at[3], f_r.at[0], r, sib)
    arrive(later & (k == 1), f10, f_r.at[0])
    for a in range(3, A):
        row_tile(a)

    row_other(0)
    for b in range(TC):
        row_b = (b * C + c) % R

        @pl.when(r == row_b)
        def _():
            colf[b] = rowf[:, 0]
        for kk in range(2):
            at = b * 2 + kk
            ref = colf.at[b, kk]
            arrive(r != row_b, ref, c_r.at[at])
            send((r != row_b) & (x == k), ref, ref, cx_s.at[at], c_r.at[at], mate, c)

    @pl.when(lead & (k == 1))
    def _():
        f10[...] = colf[0, 0]
    send(lead & (k == 1), colf.at[0, 0], f10, fx_s.at[4], f_r.at[0], r, sib)
    arrive(lead & (k == 0), f10, f_r.at[0])

    sample_own(lead)
    got = sbuf.at[1 - x, mine]
    arrive(true, got, s_r.at[1 - x])
    send(true, got, got, s_s.at[4], sb_r.at[1 - x], r, sib)

    w0, w1 = w[0], w[1]
    l01[...] = dot_nn(f10[...], w0).astype(BF16)
    for b in range(TC):
        j = b * C + c
        f0 = (j >= 1).astype(F32)
        f1 = (j >= 2).astype(F32)
        c0 = (dot_nn(colf[b, 0], w0) * f0).astype(BF16)
        u = (colf[b, 1].astype(F32) - dot_nt(c0, l01[...])).astype(BF16)
        c1 = (dot_nn(u, w1) * f1).astype(BF16)
        cols[b, :, 0:B] = c0
        cols[b, :, B:2 * B] = c1

    arrive(q > 0, sbuf.at[x, other], sb_r.at[x])
    arrive(true, sbuf.at[1 - x, other], sb_r.at[1 - x])
    w0t = w0.astype(F32).T.astype(BF16)
    w1t = w1.astype(F32).T.astype(BF16)
    y0 = dot_nn(w0t, sbuf[0]).astype(BF16)
    ys[0:B, :] = y0
    r1 = (sbuf[1].astype(F32) - dot_nn(l01[...], y0)).astype(BF16)
    ys[B:2 * B, :] = dot_nn(w1t, r1).astype(BF16)

    for a in range(1, A):
        row_other(a)

    def tile_row(a, carry):
        i = a * R + r
        f0 = (i >= 1).astype(F32)
        f1 = (i >= 2).astype(F32)
        p0 = (dot_nn(rowf[0, a], w[0]) * f0).astype(BF16)
        u = (rowf[1, a].astype(F32) - dot_nt(p0, l01[...])).astype(BF16)
        p1 = (dot_nn(u, w[1]) * f1).astype(BF16)
        rows[:, 0:B] = p0
        rows[:, B:2 * B] = p1
        for b in range(TC):
            out[a, b] = (fm[a, b].astype(F32) - dot_nt(rows[...], cols[b])).astype(BF16)
        sol[a] = (smp[a].astype(F32) - dot_nn(rows[...], ys[...])).astype(BF16)

        @pl.when((c == 0) & (i >= 1))
        def _():
            out[a, 0] = p0

        @pl.when((c == 0) & (i < 1))
        def _():
            out[a, 0] = rowf[0, a]

        @pl.when((c == 1) & (i >= 2))
        def _():
            out[a, 0] = p1

        @pl.when((c == 1) & (i < 2))
        def _():
            out[a, 0] = u

        @pl.when(i == 0)
        def _():
            sol[a] = ys[0:B, :]

        @pl.when(i == 1)
        def _():
            sol[a] = ys[B:2 * B, :]
        return carry

    lax.fori_loop(0, A, tile_row, 0)

    for cond, copy in pending:
        @pl.when(cond)
        def _():
            copy.wait_send()


def body(R, C, front_tiles, fill_pattern, w_inverse, samples):
    A, B, TC, _ = front_tiles.shape
    S = samples.shape[2]
    assert R % 2 == 0 and C % 2 == 0 and TC * C <= R and TC <= 2
    on = fill_pattern.reshape(A, 1, TC, 1) != 0
    zero = jnp.zeros((), BF16)
    fm = jnp.where(on, front_tiles, zero).transpose(0, 2, 1, 3)
    dma = pltpu.SemaphoreType.DMA
    vmem = pl.BlockSpec(memory_space=pltpu.VMEM)
    out, sol = pl.pallas_call(
        functools.partial(kernel, R, C),
        out_shape=(jax.ShapeDtypeStruct((A, TC, B, B), BF16), jax.ShapeDtypeStruct((A, B, S), BF16)),
        in_specs=[vmem] * 3,
        out_specs=(vmem, vmem),
        scratch_shapes=[
            pltpu.VMEM((2, A, B, B), BF16),
            pltpu.VMEM((TC, 2, B, B), BF16),
            pltpu.VMEM((B, B), BF16),
            pltpu.VMEM((2, B, S), BF16),
            pltpu.VMEM((TC, B, 2 * B), BF16),
            pltpu.VMEM((B, 2 * B), BF16),
            pltpu.VMEM((2 * B, S), BF16),
            pltpu.VMEM((B, B), BF16),
            dma((A,)), dma((A,)), dma((A,)), dma((A,)),
            dma((R // 2,)), dma((2 * TC,)), dma((2 * TC,)),
            dma((R // 2,)), dma((5,)), dma((1,)),
            dma((R // 2,)), dma((5,)), dma((2,)), dma((2,)),
        ],
        compiler_params=pltpu.CompilerParams(
            collective_id=0, has_side_effects=True, vmem_limit_bytes=32 * 1024 * 1024),
        name="panels",
    )(fm, w_inverse, samples)
    factor = jnp.where(on, out.transpose(0, 2, 1, 3), zero)
    return factor, sol


def solution(mesh):
    R, C = mesh.shape["row"], mesh.shape["col"]
    in_specs = (P(None, "row", None, "col"), P(None, "row", None, "col"), P(), P(None, "row", None))
    out_specs = (P(None, "row", None, "col"), P(None, "row", None))
    return jax.shard_map(functools.partial(body, R, C), mesh=mesh, in_specs=in_specs,
                         out_specs=out_specs, check_vma=False)
```

```python
import functools

import jax
import jax.numpy as jnp
from jax import lax
from jax.experimental import pallas as pl
from jax.experimental.pallas import tpu as pltpu
from jax.sharding import PartitionSpec as P

MESH = pl.DeviceIdType.MESH
F32 = jnp.float32
BF16 = jnp.bfloat16


def dot_nn(a, b):
    return jnp.dot(a, b, preferred_element_type=F32)


def dot_nt(a, b):
    return lax.dot_general(a, b, (((1,), (1,)), ((), ())), preferred_element_type=F32)


def kernel(R, C, fm, w, smp, out, sol, rowf, colf, f10, sbuf, cols, rows, ys, l01,
           y_s, y_r, b_s, b_r, cz_s, cx_s, c_r, fz_s, fx_s, f_r, sz_s, s_s, s_r, sb_r):
    A, TC, B, _ = fm.shape
    Q = R // 2
    Y = C // 2
    half = B // 2
    r, c = lax.axis_index("row"), lax.axis_index("col")
    q, x, yy, k = r // 2, r % 2, c // 2, c % 2
    sib = c + 1 - 2 * k
    mate = r + 1 - 2 * x
    line_col = 2 * yy + x
    pending = []

    def desc(src, dst, ss, rs, row, col):
        return pltpu.make_async_remote_copy(
            src_ref=src, dst_ref=dst, send_sem=ss, recv_sem=rs,
            device_id={"row": row, "col": col}, device_id_type=MESH)

    def send(cond, src, dst, ss, rs, row, col):
        copy = desc(src, dst, ss, rs, row, col)
        pending.append((cond, copy))

        @pl.when(cond)
        def _():
            copy.start()

    def arrive(cond, dst, rs):
        @pl.when(cond)
        def _():
            desc(dst, dst, fx_s.at[0], rs, r, sib).wait_recv()

    step = [jnp.where(2 * q < Q, Q - d, d) for d in range(1, Q)]
    away_rows = [2 * lax.rem(q + d, Q) + x for d in step]

    strides = [2 ** t for t in reversed(range(Q.bit_length() - 1))]

    def tree_sends(cond, src, dst, ss, rs):
        for n, stride in enumerate(strides):
            send(cond & (q % (2 * stride) == 0), src, dst, ss.at[n], rs, r + 2 * stride, c)

    barrier = pltpu.get_barrier_semaphore()
    has_yu, has_yd = yy + 1 < Y, yy > 0
    true = r >= 0
    peers = [(true, r, sib), (true, mate, c), (true, mate, sib)]
    for row in (r, mate):
        peers += [(has_yu, row, c + 2), (has_yd, row, c - 2)]
    for row in away_rows:
        peers += [(true, row, c), (true, row, sib)]
    for cond, row, col in peers:
        @pl.when(cond)
        def _():
            pl.semaphore_signal(barrier, inc=1, device_id={"row": row, "col": col}, device_id_type=MESH)
    ends = (yy + 1 < Y).astype(jnp.int32) + (yy > 0).astype(jnp.int32)
    pl.semaphore_wait(barrier, 3 + 2 * (Q - 1) + 2 * ends)

    lead = yy == 0
    later = yy > 0

    for a in range(A):
        send(lead & has_yu, fm.at[a, 0], rowf.at[k, a], y_s.at[a], y_r.at[a], r, c + 2)

    @pl.when(lead)
    def _():
        rowf[k, 0] = fm[0, 0]

    root_b = r // C
    root = (r < TC * C) & ((r % C) // 2 == yy)
    put_b = jnp.where(root, root_b, 0)
    put = colf.at[put_b, k]
    put_sem = c_r.at[put_b * 2 + k]
    f_root = later & (r == 1) & (k == 0)

    def root_sends(cond):
        for n, row in enumerate(away_rows):
            send(cond & root, rowf.at[k, 0], put, cz_s.at[n], put_sem, row, line_col)
        send(cond & root, rowf.at[k, 0], put, cz_s.at[Q - 1], put_sem, mate, line_col)

    def row_tile(a):
        arrive(later, rowf.at[k, a], y_r.at[a])
        send(later, rowf.at[k, a], rowf.at[k, a], b_s.at[a], b_r.at[a], r, sib)
        send(later & has_yu, rowf.at[k, a], rowf.at[k, a], y_s.at[a], y_r.at[a], r, c + 2)

    def row_other(a):
        arrive(true, rowf.at[1 - k, a], b_r.at[a])

    root_sends(lead)
    for a in range(A):
        send(lead, fm.at[a, 0], rowf.at[k, a], b_s.at[a], b_r.at[a], r, sib)

    mine = pl.ds(pl.multiple_of(k * half, half), half)
    other = pl.ds(pl.multiple_of((1 - k) * half, half), half)
    top = yy == Y - 1
    s_root = q == 0
    piece = smp.at[0, mine]
    tree_sends(s_root & top, piece, sbuf.at[x, mine], sz_s, s_r.at[x])
    send(s_root, piece, sbuf.at[x, mine], s_s.at[0], s_r.at[x], mate, c)

    @pl.when(s_root)
    def _():
        sbuf[x] = smp[0]

    @pl.when(lead)
    def _():
        for a in range(1, A):
            rowf[k, a] = fm[a, 0]

    row_tile(0)
    root_sends(later)

    send(f_root, rowf.at[0, 0], f10, fx_s.at[0], f_r.at[0], mate, c)
    for n, row in enumerate(away_rows):
        send(f_root, rowf.at[0, 0], f10, fz_s.at[n], f_r.at[0], row, c)
    send(f_root, rowf.at[0, 0], f10, fx_s.at[1], f_r.at[0], r, sib)

    @pl.when(f_root)
    def _():
        f10[...] = rowf[0, 0]

    def sample_own(cond):
        got = sbuf.at[x, mine]
        cond = cond & (q > 0)
        arrive(cond, got, s_r.at[x])
        tree_sends(cond & top, got, got, sz_s, s_r.at[x])
        send(cond & has_yd, got, got, s_s.at[2], s_r.at[x], r, c - 2)
        send(cond & has_yd, got, got, s_s.at[1], s_r.at[x], mate, c - 2)
        send(cond & top, got, got, s_s.at[0], s_r.at[x], mate, c)
        send(cond, got, got, s_s.at[3], sb_r.at[x], r, sib)

    def col_items(b, cond):
        row_b = (b * C + c) % R
        here = cond & (r == row_b)

        @pl.when(here)
        def _():
            colf[b] = rowf[:, 0]
        away = cond & (r != row_b)
        for kk in range(2):
            at = b * 2 + kk
            ref = colf.at[b, kk]
            arrive(away, ref, c_r.at[at])
            send(away & (x == k), ref, ref, cx_s.at[at], c_r.at[at], mate, c)

    sample_own(later)
    if A > 1:
        row_tile(1)

    near = later & (k == 0) & ((x == 1) | (r == 0))
    arrive(near & (r != 1), f10, f_r.at[0])
    for n, row in enumerate(away_rows):
        send(near & (r == 0), f10, f10, fz_s.at[n], f_r.at[0], row, c)
    send(near & (r != 1), f10, f10, fx_s.at[3], f_r.at[0], r, sib)
    for a in range(2, A):
        row_tile(a)

    row_other(0)
    for b in range(TC):
        col_items(b, (x == k))
    col_items(0, lead & (x != k))

    @pl.when(lead & (k == 1))
    def _():
        f10[...] = colf[0, 0]
    send(lead & (k == 1), colf.at[0, 0], f10, fx_s.at[4], f_r.at[0], r, sib)
    far = later & (k == 0) & (x == 0) & (r != 0)
    arrive((lead & (k == 0)) | (later & (k == 1)) | far, f10, f_r.at[0])
    send(far, f10, f10, fx_s.at[3], f_r.at[0], r, sib)
    for a in range(1, A):
        row_other(a)

    l01[...] = dot_nn(f10[...], w[0]).astype(BF16)

    def panel(a, carry):
        i = a * R + r
        f0 = (i >= 1).astype(F32)
        f1 = (i >= 2).astype(F32)
        p0 = (dot_nn(rowf[0, a], w[0]) * f0).astype(BF16)
        u = (rowf[1, a].astype(F32) - dot_nt(p0, l01[...])).astype(BF16)
        p1 = (dot_nn(u, w[1]) * f1).astype(BF16)
        rows[a, :, 0:B] = p0
        rows[a, :, B:2 * B] = p1

        @pl.when((c == 0) & (i >= 1))
        def _():
            out[a, 0] = p0

        @pl.when((c == 0) & (i < 1))
        def _():
            out[a, 0] = rowf[0, a]

        @pl.when((c == 1) & (i >= 2))
        def _():
            out[a, 0] = p1

        @pl.when((c == 1) & (i < 2))
        def _():
            out[a, 0] = u
        return carry

    lax.fori_loop(0, A, panel, 0)

    sample_own(lead)
    got = sbuf.at[1 - x, mine]
    arrive(true, got, s_r.at[1 - x])
    send(true, got, got, s_s.at[4], sb_r.at[1 - x], r, sib)

    arrive(q > 0, sbuf.at[x, other], sb_r.at[x])
    arrive(true, sbuf.at[1 - x, other], sb_r.at[1 - x])
    w0t = w[0].astype(F32).T.astype(BF16)
    w1t = w[1].astype(F32).T.astype(BF16)
    y0 = dot_nn(w0t, sbuf[0]).astype(BF16)
    ys[0:B, :] = y0
    r1 = (sbuf[1].astype(F32) - dot_nn(l01[...], y0)).astype(BF16)
    ys[B:2 * B, :] = dot_nn(w1t, r1).astype(BF16)

    def solve(a, carry):
        i = a * R + r
        sol[a] = (smp[a].astype(F32) - dot_nn(rows[a], ys[...])).astype(BF16)

        @pl.when(i == 0)
        def _():
            sol[a] = ys[0:B, :]

        @pl.when(i == 1)
        def _():
            sol[a] = ys[B:2 * B, :]
        return carry

    lax.fori_loop(0, A, solve, 0)

    col_items(0, later & (x != k))
    for b in range(1, TC):
        col_items(b, x != k)

    for b in range(TC):
        j = b * C + c
        f0 = (j >= 1).astype(F32)
        f1 = (j >= 2).astype(F32)
        c0 = (dot_nn(colf[b, 0], w[0]) * f0).astype(BF16)
        u = (colf[b, 1].astype(F32) - dot_nt(c0, l01[...])).astype(BF16)
        c1 = (dot_nn(u, w[1]) * f1).astype(BF16)
        cols[b, :, 0:B] = c0
        cols[b, :, B:2 * B] = c1

    def trail(a, carry):
        for b in range(TC):
            part = (fm[a, b].astype(F32) - dot_nt(rows[a], cols[b])).astype(BF16)
            if b > 0:
                out[a, b] = part
            else:
                @pl.when(c >= 2)
                def _():
                    out[a, b] = part
        return carry

    lax.fori_loop(0, A, trail, 0)

    for cond, copy in pending:
        @pl.when(cond)
        def _():
            copy.wait_send()


def body(R, C, front_tiles, fill_pattern, w_inverse, samples):
    A, B, TC, _ = front_tiles.shape
    S = samples.shape[2]
    assert R % 2 == 0 and C % 2 == 0 and TC * C <= R and (R & (R - 1)) == 0
    on = fill_pattern.reshape(A, 1, TC, 1) != 0
    zero = jnp.zeros((), BF16)
    fm = jnp.where(on, front_tiles, zero).transpose(0, 2, 1, 3)
    dma = pltpu.SemaphoreType.DMA
    vmem = pl.BlockSpec(memory_space=pltpu.VMEM)
    out, sol = pl.pallas_call(
        functools.partial(kernel, R, C),
        out_shape=(jax.ShapeDtypeStruct((A, TC, B, B), BF16), jax.ShapeDtypeStruct((A, B, S), BF16)),
        in_specs=[vmem] * 3,
        out_specs=(vmem, vmem),
        scratch_shapes=[
            pltpu.VMEM((2, A, B, B), BF16),
            pltpu.VMEM((TC, 2, B, B), BF16),
            pltpu.VMEM((B, B), BF16),
            pltpu.VMEM((2, B, S), BF16),
            pltpu.VMEM((TC, B, 2 * B), BF16),
            pltpu.VMEM((A, B, 2 * B), BF16),
            pltpu.VMEM((2 * B, S), BF16),
            pltpu.VMEM((B, B), BF16),
            dma((A,)), dma((A,)), dma((A,)), dma((A,)),
            dma((R // 2,)), dma((2 * TC,)), dma((2 * TC,)),
            dma((R // 2,)), dma((5,)), dma((1,)),
            dma((R // 2,)), dma((5,)), dma((2,)), dma((2,)),
        ],
        compiler_params=pltpu.CompilerParams(
            collective_id=0, has_side_effects=True, vmem_limit_bytes=32 * 1024 * 1024),
        name="panels",
    )(fm, w_inverse, samples)
    factor = jnp.where(on, out.transpose(0, 2, 1, 3), zero)
    return factor, sol


def solution(mesh):
    R, C = mesh.shape["row"], mesh.shape["col"]
    in_specs = (P(None, "row", None, "col"), P(None, "row", None, "col"), P(), P(None, "row", None))
    out_specs = (P(None, "row", None, "col"), P(None, "row", None))
    return jax.shard_map(functools.partial(body, R, C), mesh=mesh, in_specs=in_specs,
                         out_specs=out_specs, check_vma=False)
```
